32 devices in a mesh: grp: 2 (over x), bus: 16 (over z, y, core).
Axes of the slice: x: 2, y: 2, z: 4, core: 2. Of those that a mesh axis runs over, the one named last changes fastest.
Arguments:
- loads: float32 [16384, 128], P(('grp', 'bus')), parts along dimension 0, may hold values from -4 to 4
- bus_type: int32 [16384], P(('grp', 'bus')), parts along dimension 0, may hold values from 0 to 2
- bus_slot: int32 [16384], P(('grp', 'bus')), parts along dimension 0, may hold values from 0 to 511, as said below
- block_inverse: float32 [128, 2, 128, 128], P(('grp', 'bus')), parts along dimension 0, may hold values from -1.5 to 1.5
- schur_inverse: float32 [2, 2048, 1024], P(None, ('grp', 'bus')), parts along dimension 1, may hold values from -1.5 to 1.5
- branch_bus: int32 [8192], P(('grp', 'bus')), parts along dimension 0, may hold values from 0 to 511
- branch_iface: int32 [8192], P(('grp', 'bus')), parts along dimension 0, may hold values from 0 to 1023, as said below
- branch_adm: float32 [2, 8192], P(None, ('grp', 'bus')), parts along dimension 1, may hold values from -4 to 4
Outputs:
- voltage: float32 [16384, 128], P(('grp', 'bus')), parts along dimension 0
- last_term: float32 [16384, 128], P(('grp', 'bus')), parts along dimension 0
The draws below stay inside these ranges and needn't reach their ends.
There are 2 independent parts, one for each index of `grp`. The reference program is written for one: setup_inputs(seed, part) draws one part's arguments, and reference() takes and returns one part's arrays. A program takes and returns all parts, laid end to end along the dimension named above; each array names one. Nothing has to cross between parts.
Inputs may be any that keep to these rules, and one draw needn't show every extreme that they name: Within each device's 4 * 128 buses, bus_slot is a permutation of 0 to 511. `branch_iface`: A branch of device d names an interface row from max(d - 1, 0) * 64 to min(d + 2, 16) * 64 - 1.
All inputs are finite; a program needn't handle non-finite values.
Results may differ from the reference program's by a relative error of at most 0.00027.
Values sent between devices are 32-bit elements; how exact they have to be, the bound alone decides.
A program may use at most 64 MiB of HBM per device.

```python
import jax
import jax.numpy as jnp
from jax import lax

PB = 128
IF_DEV = 64
PART_DEV = 4
SCEN = 64
BR_DEV = 256
ORDERS = 4
BUSES = 8192
PARTS_SIZE = 64
IFACE = 1024
BRANCHES = 4096


def draw_bus_slot(key, part):
    key = jax.random.fold_in(key, 1)
    bus_rows = PART_DEV * PB
    blocks = BUSES // bus_rows
    keys = jax.random.split(key, blocks)

    def shuffle(one_key):
        return jax.random.permutation(one_key, bus_rows)
    return jax.vmap(shuffle)(keys).reshape(-1).astype(jnp.int32)


def draw_block_inverse(key, part):
    key = jax.random.fold_in(key, 2)
    key_off, key_diag = jax.random.split(key, 2)
    shape = (PARTS_SIZE, 2, PB, PB)
    offdiag = jax.random.normal(key_off, shape, jnp.float32) * (0.5 / PB ** 0.5)
    diagonal = jax.random.uniform(key_diag, (PARTS_SIZE, 1, PB, 1), jnp.float32, 0.8, 1.2)
    identity = (jnp.arange(PB)[:, None] == jnp.arange(PB)[None, :]).astype(jnp.float32)[None, None]
    is_real = (jnp.arange(2) == 0).astype(jnp.float32).reshape(1, 2, 1, 1)
    return offdiag * (1.0 - identity) + identity * diagonal * is_real


def draw_schur_inverse(key, part):
    key = jax.random.fold_in(key, 3)
    key_off, key_diag = jax.random.split(key, 2)
    shape = (2, IFACE, IFACE)
    offdiag = jax.random.normal(key_off, shape, jnp.float32) * (0.5 / IFACE ** 0.5)
    diagonal = jax.random.uniform(key_diag, (1, IFACE, 1), jnp.float32, 0.8, 1.2)
    identity = (jnp.arange(IFACE)[:, None] == jnp.arange(IFACE)[None, :]).astype(jnp.float32)[None]
    is_real = (jnp.arange(2) == 0).astype(jnp.float32).reshape(2, 1, 1)
    return offdiag * (1.0 - identity) + identity * diagonal * is_real


def draw_branch_iface(key, part):
    key = jax.random.fold_in(key, 4)
    blocks = IFACE // IF_DEV
    device = jnp.arange(BRANCHES, dtype=jnp.int32) // BR_DEV
    lowest = jnp.maximum(device - 1, 0) * IF_DEV
    highest_row = jnp.minimum(device + 2, blocks) * IF_DEV
    drawn = jax.random.randint(key, (BRANCHES,), lowest, highest_row)
    within = jnp.arange(BRANCHES, dtype=jnp.int32) % BR_DEV
    drawn = jnp.where(within == 0, lowest, jnp.where(within == 1, highest_row - 1, drawn))
    return drawn.astype(jnp.int32)


def with_ends(values, rng, smallest, top_value):
    place = [jax.random.randint(jax.random.fold_in(rng, axis), (), 0, length) for axis, length in enumerate(values.shape)]
    widest = values.shape.index(max(values.shape))
    beside = place[:widest] + [(place[widest] + 1) % values.shape[widest]] + place[widest + 1:]
    return values.at[tuple(place)].set(smallest).at[tuple(beside)].set(top_value)


def steps_of(key, shape, cuts, smallest, high):
    level, own = 1.0, jax.random.fold_in(key, 6)
    for axis_at, blocks in cuts:
        steps = jnp.exp(jax.random.uniform(jax.random.fold_in(own, axis_at), (blocks,), jnp.float32, smallest / len(cuts), high / len(cuts)))
        level = level * jnp.repeat(steps, shape[axis_at] // blocks).reshape([-1 if axis == axis_at else 1 for axis in range(len(shape))])
    return level


def centred(key, extent, scale, bound, pieces=(), kind=jnp.bfloat16):
    loudness = steps_of(key, extent, pieces, -0.22, 0.18) if pieces else 1.0
    result = jax.random.normal(key, extent, jnp.float32) * scale * loudness
    return jnp.minimum(jnp.maximum(result, -bound), bound).astype(kind)


def setup_inputs(seed: int = 0, part: int = 0) -> dict:
    streams_of = jax.random.split(jax.random.key(seed), 9)
    part_keys = jax.random.split(jax.random.fold_in(streams_of[8], part), 9)
    loads = centred(part_keys[0], (BUSES, 2 * SCEN), 0.5, 4.0, ((0, 16),), jnp.float32)
    bus_type = with_ends(jax.random.randint(part_keys[1], (BUSES,), 0, 3), jax.random.fold_in(part_keys[1], 1), 0, 2).astype(jnp.int32)
    bus_slot = draw_bus_slot(jax.random.fold_in(jax.random.fold_in(streams_of[8], part), 71), part)
    block_inverse = draw_block_inverse(jax.random.fold_in(jax.random.fold_in(streams_of[8], part), 71), part)
    schur_inverse = draw_schur_inverse(jax.random.fold_in(jax.random.fold_in(streams_of[8], part), 71), part)
    branch_bus = with_ends(jax.random.randint(part_keys[5], (BRANCHES,), 0, PART_DEV * PB), jax.random.fold_in(part_keys[5], 1), 0, (PART_DEV * PB) - 1).astype(jnp.int32)
    branch_iface = draw_branch_iface(jax.random.fold_in(jax.random.fold_in(streams_of[8], part), 71), part)
    branch_adm = centred(part_keys[7], (2, BRANCHES), 0.7, 4.0, ((1, 16),), jnp.float32)
    return dict(loads=loads, bus_type=bus_type, bus_slot=bus_slot, block_inverse=block_inverse, schur_inverse=schur_inverse, branch_bus=branch_bus, branch_iface=branch_iface, branch_adm=branch_adm)


highest = lax.Precision.HIGHEST


def complex_mul(first, second):
    width = first.shape[-1] // 2
    first_real, first_imag = first[..., :width], first[..., width:]
    second_real, second_imag = second[..., :width], second[..., width:]
    return jnp.concatenate([first_real * second_real - first_imag * second_imag,
                            first_real * second_imag + first_imag * second_real], axis=-1)


def conjugate(values):
    width = values.shape[-1] // 2
    return jnp.concatenate([values[..., :width], -values[..., width:]], axis=-1)


def rotate(values):
    width = values.shape[-1] // 2
    return jnp.concatenate([-values[..., width:], values[..., :width]], axis=-1)


def admit(values, adm_real, adm_imag):
    return values * adm_real + rotate(values) * adm_imag


def block_solve(inverse, right_side):
    count, rows = inverse.shape[0], inverse.shape[2]
    blocks = right_side.reshape(count, rows, right_side.shape[-1])
    real_term = jnp.einsum('pij,pjc->pic', inverse[:, 0], blocks, precision=highest, preferred_element_type=jnp.float32)
    imag_term = jnp.einsum('pij,pjc->pic', inverse[:, 1], blocks, precision=highest, preferred_element_type=jnp.float32)
    return (real_term + rotate(imag_term)).reshape(count * rows, right_side.shape[-1])


def reference(loads, bus_type, bus_slot, block_inverse, schur_inverse, branch_bus, branch_iface, branch_adm):
    bus_rows = PART_DEV * PB
    device_base = (jnp.arange(BUSES, dtype=jnp.int32) // bus_rows) * bus_rows
    global_slot = (device_base + bus_slot).astype(jnp.int32)
    placed_loads = jnp.zeros_like(loads).at[global_slot].set(loads)
    placed_type = jnp.zeros_like(bus_type).at[global_slot].set(bus_type)
    branch_base = (jnp.arange(BRANCHES, dtype=jnp.int32) // BR_DEV) * bus_rows
    branch_pos = global_slot[(branch_base + branch_bus).astype(jnp.int32)]
    adm_real = branch_adm[0][:, None]
    adm_imag = branch_adm[1][:, None]
    unit = jnp.concatenate([jnp.ones((BUSES, SCEN), jnp.float32), jnp.zeros((BUSES, SCEN), jnp.float32)], axis=-1)
    load_mask = (placed_type == 0)[:, None]
    current_mask = (placed_type == 1)[:, None]
    coeffs = [unit]
    inverses = [unit]
    for degree in range(1, ORDERS + 1):
        driven = jnp.where(load_mask, conjugate(complex_mul(placed_loads, inverses[-1])), 0.0)
        if degree == 1:
            driven = driven + jnp.where(current_mask, conjugate(placed_loads), 0.0)
        local_solution = block_solve(block_inverse, driven)
        flows = admit(local_solution[branch_pos], adm_real, adm_imag)
        sums = jax.ops.segment_sum(flows, branch_iface, num_segments=IFACE)
        interface = jnp.dot(schur_inverse[0], sums, precision=highest, preferred_element_type=jnp.float32)
        interface = interface + rotate(jnp.dot(schur_inverse[1], sums, precision=highest, preferred_element_type=jnp.float32))
        returned = jax.ops.segment_sum(admit(interface[branch_iface], adm_real, adm_imag), branch_pos, num_segments=BUSES)
        coeff = block_solve(block_inverse, driven + returned)
        coeffs.append(coeff)
        total = complex_mul(coeffs[1], inverses[degree - 1])
        for inner in range(2, degree + 1):
            total = total + complex_mul(coeffs[inner], inverses[degree - inner])
        inverses.append(-total)
    voltage = coeffs[0]
    for inner in range(1, ORDERS + 1):
        voltage = voltage + coeffs[inner]
    return voltage[global_slot], coeffs[-1][global_slot]
```

```python
import functools

import jax
import jax.numpy as jnp
from jax import lax
from jax.experimental import pallas as pl
from jax.experimental.pallas import tpu as pltpu
from jax.sharding import PartitionSpec as P

ORDERS = 4
INNER = 4
F32 = jnp.float32
BF16 = jnp.bfloat16
MESH = pl.DeviceIdType.MESH


def dot(a, b):
    return lax.dot_general(a, b, (((1,), (0,)), ((), ())), preferred_element_type=F32)


def dot_nt(a, b):
    return lax.dot_general(a, b, (((1,), (1,)), ((), ())), preferred_element_type=F32)


def split(x):
    high = x.astype(BF16)
    return high, (x - high.astype(F32)).astype(BF16)


def low_half(shape):
    return lax.broadcasted_iota(jnp.int32, shape, 1) < shape[1] // 2


def swap(x):
    return pltpu.roll(x, x.shape[1] // 2, 1)


def rotate(x):
    other = swap(x)
    return jnp.where(low_half(x.shape), -other, other)


def one_sided(select, x):
    high, low = split(x)
    out = dot(select, jnp.concatenate([high, low], axis=1))
    width = x.shape[1]
    return out[:, :width] + out[:, width:]


def dot3(a, b, mul):
    a_high, a_low = split(a)
    b_high, b_low = split(b)
    return mul(a_high, b_high) + (mul(a_high, b_low) + mul(a_low, b_high))


def complex_apply(high, low, x):
    width = x.shape[1]
    x_high, x_low = split(x)
    both = dot(high, jnp.concatenate([x_high, x_low], axis=1))
    out = both[:, :width] + (both[:, width:] + dot(low, x_high))
    rows = out.shape[0] // 2
    return out[:rows] + rotate(out[rows:])


def complex_mul(a, b):
    other = swap(a)
    low = low_half(a.shape)
    real = jnp.where(low, a, other)
    imag = jnp.where(low, -other, a)
    return real * b + imag * swap(b)


def kernel(
    n,
    loads, types, slots, block_inverse, schur, branch_bus, branch_iface, adm,
    voltage_out, last_out,
    perm, drv, mul_same, mul_swap, w_high, w_low, h_high, h_low, b_high, b_low,
    s_win, s_high, s_low, coeffs, terms, near, nb, gath,
    own_sem, s_send, s_recv, nb_send, nb_recv, z_send, z_recv, y_send, y_recv,
    c_send, c_recv, f_send, f_recv,
):
    outer_n = n // INNER
    me = lax.axis_index("bus")
    outer = me // INNER
    inner = me % INNER
    sib = me + 1 - 2 * (me % 2)
    pair = me + 2 - 4 * ((me // 2) % 2)
    pair_inner = pair % INNER
    bus_rows, columns = loads.shape
    if_rows = schur.shape[1]
    parts, pb = block_inverse.shape[0], block_inverse.shape[2]
    rows3 = 3 * if_rows
    pad = h_high.shape[1]

    def remote(src, dst, send, recv, device):
        return pltpu.make_async_remote_copy(
            src_ref=src, dst_ref=dst, send_sem=send, recv_sem=recv,
            device_id={"bus": device}, device_id_type=MESH,
        )

    def has_prev(fn):
        pl.when(me > 0)(fn)

    def has_next(fn):
        pl.when(me < n - 1)(fn)

    barrier = pltpu.get_barrier_semaphore()

    def greet(device):
        pl.semaphore_signal(barrier, inc=1, device_id={"bus": device}, device_id_type=MESH)

    has_prev(lambda: greet(me - 1))
    has_next(lambda: greet(me + 1))
    for j in range(1, outer_n):
        greet(((outer + j) % outer_n) * INNER + inner)
    greet(sib)
    greet(pair)
    own_copy = pltpu.make_async_copy(schur, s_win.at[1], own_sem)
    own_copy.start()
    edges = jnp.where(me > 0, 1, 0) + jnp.where(me < n - 1, 1, 0)
    pl.semaphore_wait(barrier, outer_n + 1 + edges)

    to_prev = remote(schur, s_win.at[2], s_send.at[0], s_recv.at[0], me - 1)
    to_next = remote(schur, s_win.at[0], s_send.at[1], s_recv.at[1], me + 1)
    has_prev(to_prev.start)
    has_next(to_next.start)

    slot = slots[...]
    kind = types[...]
    hit = lax.broadcasted_iota(jnp.int32, (bus_rows, bus_rows), 0) == slot
    ones = jnp.where(hit, 1.0, 0.0)
    perm[...] = ones.T.astype(BF16)
    place = ones.astype(BF16)
    load_place = jnp.where(kind == 0, ones, 0.0).astype(BF16)
    first_place = jnp.where(kind <= 1, ones, 0.0).astype(BF16)
    placed = one_sided(load_place, loads[...])
    first = one_sided(first_place, loads[...])
    low = low_half((bus_rows, columns))
    drv[...] = jnp.where(low, first, -first)
    other = swap(placed)
    mul_same[...] = jnp.where(low, -placed, other)
    mul_swap[...] = jnp.where(low, other, placed)

    branches = branch_bus.shape[1]
    at_bus = lax.broadcasted_iota(jnp.int32, (bus_rows, branches), 0) == branch_bus[...]
    spread = dot(place, jnp.where(at_bus, 1.0, 0.0).astype(BF16)).astype(BF16)
    relative = branch_iface[...] - (me - 1) * if_rows
    at_row = lax.broadcasted_iota(jnp.int32, (pad, branches), 0) == relative
    weights = jnp.concatenate(
        [jnp.where(at_row, adm[0:1, :], 0.0), jnp.where(at_row, adm[1:2, :], 0.0)], axis=0
    )
    weights_high, weights_low = split(weights)
    joins = dot_nt(weights_high, spread) + dot_nt(weights_low, spread)
    for p in range(parts):
        cols = slice(p * pb, (p + 1) * pb)
        inv_re, inv_im = block_inverse[p, 0], block_inverse[p, 1]
        high, lowp = split(jnp.concatenate([inv_re, inv_im], axis=0))
        b_high[p] = high
        b_low[p] = lowp
        g = joins[:, cols]
        q = dot3(g, jnp.concatenate([inv_re, inv_im], axis=1), dot)
        w_re = q[:rows3, :pb] - q[pad : pad + rows3, pb:]
        w_im = q[:rows3, pb:] + q[pad : pad + rows3, :pb]
        high, lowp = split(jnp.concatenate([w_re, w_im], axis=0))
        w_high[:, cols] = high
        w_low[:, cols] = lowp
        r = dot3(jnp.concatenate([inv_re, inv_im], axis=0), g, dot_nt)
        high, lowp = split(r[:pb, :pad] - r[pb:, pad:])
        h_high[p * pb : (p + 1) * pb, :] = high
        h_low[p * pb : (p + 1) * pb, :] = lowp
        high, lowp = split(r[:pb, pad:] + r[pb:, :pad])
        at = bus_rows + p * pb
        h_high[at : at + pb, :] = high
        h_low[at : at + pb, :] = lowp

    @pl.when(me == 0)
    def _():
        s_win[0] = jnp.zeros(s_win.shape[1:], F32)
        nb[:, 0] = jnp.zeros((ORDERS, if_rows, columns), F32)

    @pl.when(me == n - 1)
    def _():
        s_win[2] = jnp.zeros(s_win.shape[1:], F32)
        nb[:, 1] = jnp.zeros((ORDERS, if_rows, columns), F32)

    def order(t, carry):
        x = drv[...]
        near[t] = complex_apply(w_high[...], w_low[...], x)
        lower = remote(
            near.at[t, pl.ds(0, if_rows)], nb.at[t, 1], nb_send.at[t, 0], nb_recv.at[t, 0], me - 1
        )
        upper = remote(
            near.at[t, pl.ds(2 * if_rows, if_rows)],
            nb.at[t, 0], nb_send.at[t, 1], nb_recv.at[t, 1], me + 1,
        )
        has_prev(lower.start)
        has_next(upper.start)
        for p in range(parts):
            at = slice(p * pb, (p + 1) * pb)
            coeffs[t, at, :] = complex_apply(b_high[p], b_low[p], x[at])
        has_next(lower.wait_recv)
        has_prev(upper.wait_recv)
        gath[t, me] = near[t, if_rows : 2 * if_rows, :] + (nb[t, 0] + nb[t, 1])

        sends = []
        z_copies = []
        for j in range(1, outer_n):
            to = ((outer + j) % outer_n) * INNER + inner
            block = gath.at[t, me]
            copy = remote(block, block, z_send.at[t, j], z_recv.at[t, j], to)
            copy.start()
            z_copies.append(copy)
        y_copies = []
        for j in range(outer_n):
            if j:
                z_copies[j - 1].wait_recv()
            came = ((outer - j + outer_n) % outer_n) * INNER + inner
            block = gath.at[t, came]
            copy = remote(block, block, y_send.at[t, j], y_recv.at[t, j], pair)
            copy.start()
            y_copies.append(copy)
            copy = remote(block, block, c_send.at[t, j], c_recv.at[t, j], sib)
            copy.start()
            sends.append(copy)

        def earlier(k, total):
            return total + complex_mul(coeffs[k], terms[t - 1 - k])

        past = lax.fori_loop(0, t, earlier, jnp.zeros((bus_rows, columns), F32))
        terms[t] = -past

        @pl.when(t == 0)
        def _():
            own_copy.wait()
            has_next(to_prev.wait_recv)
            has_prev(to_next.wait_recv)
            for part in range(2):
                for w in range(3):
                    at = (part * 3 + w) * if_rows
                    high, lowp = split(s_win[w, part])
                    s_high[at : at + if_rows, :] = high
                    s_low[at : at + if_rows, :] = lowp

        f_copies = []
        for j in range(outer_n):
            y_copies[j].wait_recv()
            came = ((outer - j + outer_n) % outer_n) * INNER + pair_inner
            block = gath.at[t, came]
            copy = remote(block, block, f_send.at[t, j], f_recv.at[t, j], sib)
            copy.start()
            f_copies.append(copy)
        for copy in sends + f_copies:
            copy.wait_recv()

        sums = gath[t].reshape(n * if_rows, columns)
        window = complex_apply(s_high[...], s_low[...], sums)
        window = jnp.concatenate([window, jnp.zeros((pad - rows3, columns), F32)], axis=0)
        coeff = coeffs[t] + complex_apply(h_high[...], h_low[...], window)
        coeffs[t] = coeff
        term = coeff + terms[t]
        terms[t] = term
        drv[...] = mul_same[...] * term + mul_swap[...] * swap(term)

        has_prev(lower.wait_send)
        has_next(upper.wait_send)
        for copy in z_copies + y_copies + sends + f_copies:
            copy.wait_send()
        return carry

    lax.fori_loop(0, ORDERS, order, 0)

    has_prev(to_prev.wait_send)
    has_next(to_next.wait_send)
    total = jnp.where(low, 1.0, 0.0)
    for k in range(ORDERS):
        total = total + coeffs[k]
    voltage_out[...] = one_sided(perm[...], total)
    last_out[...] = one_sided(perm[...], coeffs[ORDERS - 1])


def local(
    loads, bus_type, bus_slot, block_inverse, schur_inverse, branch_bus, branch_iface, branch_adm
):
    n = lax.axis_size("bus")
    bus_rows, columns = loads.shape
    if_rows, iface = schur_inverse.shape[1:]
    parts, _, pb, _ = block_inverse.shape
    outer_n = n // INNER
    rows3 = 3 * if_rows
    pad = -(-rows3 // 128) * 128
    vmem = pl.BlockSpec(memory_space=pltpu.VMEM)
    dma = pltpu.SemaphoreType.DMA
    out = jax.ShapeDtypeStruct((bus_rows, columns), F32)
    return pl.pallas_call(
        functools.partial(kernel, n),
        out_shape=(out, out),
        in_specs=[vmem, vmem, vmem, vmem, pl.BlockSpec(memory_space=pl.ANY), vmem, vmem, vmem],
        out_specs=(vmem, vmem),
        scratch_shapes=[
            pltpu.VMEM((bus_rows, bus_rows), BF16),
            pltpu.VMEM((bus_rows, columns), F32),
            pltpu.VMEM((bus_rows, columns), F32),
            pltpu.VMEM((bus_rows, columns), F32),
            pltpu.VMEM((2 * rows3, bus_rows), BF16),
            pltpu.VMEM((2 * rows3, bus_rows), BF16),
            pltpu.VMEM((2 * bus_rows, pad), BF16),
            pltpu.VMEM((2 * bus_rows, pad), BF16),
            pltpu.VMEM((parts, 2 * pb, pb), BF16),
            pltpu.VMEM((parts, 2 * pb, pb), BF16),
            pltpu.VMEM((3, 2, if_rows, iface), F32),
            pltpu.VMEM((2 * rows3, iface), BF16),
            pltpu.VMEM((2 * rows3, iface), BF16),
            pltpu.VMEM((ORDERS, bus_rows, columns), F32),
            pltpu.VMEM((ORDERS, bus_rows, columns), F32),
            pltpu.VMEM((ORDERS, rows3, columns), F32),
            pltpu.VMEM((ORDERS, 2, if_rows, columns), F32),
            pltpu.VMEM((ORDERS, n, if_rows, columns), F32),
            dma, dma((2,)), dma((2,)),
            dma((ORDERS, 2)), dma((ORDERS, 2)),
            dma((ORDERS, outer_n)), dma((ORDERS, outer_n)),
            dma((ORDERS, outer_n)), dma((ORDERS, outer_n)),
            dma((ORDERS, outer_n)), dma((ORDERS, outer_n)),
            dma((ORDERS, outer_n)), dma((ORDERS, outer_n)),
        ],
        compiler_params=pltpu.CompilerParams(
            collective_id=0, has_side_effects=True, vmem_limit_bytes=48 * 1024 * 1024
        ),
        name="power_flow",
    )(
        loads,
        bus_type.reshape(1, bus_rows),
        bus_slot.reshape(1, bus_rows),
        block_inverse,
        schur_inverse,
        branch_bus.reshape(1, -1),
        branch_iface.reshape(1, -1),
        branch_adm,
    )


def solution(mesh):
    in_specs = (
        P(("grp", "bus"), None),
        P(("grp", "bus")),
        P(("grp", "bus")),
        P(("grp", "bus"), None, None, None),
        P(None, ("grp", "bus"), None),
        P(("grp", "bus")),
        P(("grp", "bus")),
        P(None, ("grp", "bus")),
    )
    out_specs = (P(("grp", "bus"), None), P(("grp", "bus"), None))
    return jax.shard_map(local, mesh=mesh, in_specs=in_specs, out_specs=out_specs, check_vma=False)
```

```python
import functools

import jax
import jax.numpy as jnp
from jax import lax
from jax.experimental import pallas as pl
from jax.experimental.pallas import tpu as pltpu
from jax.sharding import PartitionSpec as P

ORDERS = 4
INNER = 4
CHUNKS = 16
F32 = jnp.float32
BF16 = jnp.bfloat16
MESH = pl.DeviceIdType.MESH


def dot(a, b):
    return lax.dot_general(a, b, (((1,), (0,)), ((), ())), preferred_element_type=F32)


def dot_nt(a, b):
    return lax.dot_general(a, b, (((1,), (1,)), ((), ())), preferred_element_type=F32)


def split(x):
    high = x.astype(BF16)
    return high, (x - high.astype(F32)).astype(BF16)


def low_half(shape):
    return lax.broadcasted_iota(jnp.int32, shape, 1) < shape[1] // 2


def swap(x):
    return pltpu.roll(x, x.shape[1] // 2, 1)


def rotate(x):
    other = swap(x)
    return jnp.where(low_half(x.shape), -other, other)


def one_sided(select, x):
    high, low = split(x)
    out = dot(select, jnp.concatenate([high, low], axis=1))
    width = x.shape[1]
    return out[:, :width] + out[:, width:]


def dot3(a, b, mul):
    a_high, a_low = split(a)
    b_high, b_low = split(b)
    return mul(a_high, b_high) + (mul(a_high, b_low) + mul(a_low, b_high))


def complex_apply(high, low, x):
    width = x.shape[1]
    x_high, x_low = split(x)
    both = dot(high, jnp.concatenate([x_high, x_low], axis=1))
    out = both[:, :width] + (both[:, width:] + dot(low, x_high))
    rows = out.shape[0] // 2
    return out[:rows] + rotate(out[rows:])


def complex_mul(a, b):
    other = swap(a)
    low = low_half(a.shape)
    real = jnp.where(low, a, other)
    imag = jnp.where(low, -other, a)
    return real * b + imag * swap(b)


def kernel(
    n,
    loads_in, types_in, slots_in, inverse_in, schur, bus_in, iface_in, adm_in,
    voltage_out, last_out,
    loads, types, slots, block_inverse, branch_bus, branch_iface, adm, in_sem,
    joined, own_high, own_low, own_if, window_ref, i_send, i_recv,
    perm, drv, mul_same, mul_swap, w_high, w_low, h_high, h_low, b_high, b_low,
    s_win, s_high, s_low, coeffs, terms, near, nb, gath,
    own_sem, s_send, s_recv, nb_send, nb_recv, z_send, z_recv, y_send, y_recv,
    c_send, c_recv, f_send, f_recv,
):
    outer_n = n // INNER
    me = lax.axis_index("bus")
    outer = me // INNER
    inner = me % INNER
    sib = me + 1 - 2 * (me % 2)
    pair = me + 2 - 4 * ((me // 2) % 2)
    pair_inner = pair % INNER
    bus_rows, columns = loads.shape
    if_rows = schur.shape[1]
    parts, pb = block_inverse.shape[0], block_inverse.shape[2]
    rows3 = 3 * if_rows
    pad = h_high.shape[1]

    def remote(src, dst, send, recv, device):
        return pltpu.make_async_remote_copy(
            src_ref=src, dst_ref=dst, send_sem=send, recv_sem=recv,
            device_id={"bus": device}, device_id_type=MESH,
        )

    def has_prev(fn):
        pl.when(me > 0)(fn)

    def has_next(fn):
        pl.when(me < n - 1)(fn)

    arrays = (
        (slots_in, slots), (types_in, types), (loads_in, loads), (bus_in, branch_bus),
        (iface_in, branch_iface), (adm_in, adm), (inverse_in, block_inverse),
    )
    fetches = [
        pltpu.make_async_copy(src, dst, in_sem.at[i]) for i, (src, dst) in enumerate(arrays)
    ]
    for fetch in fetches:
        fetch.start()
    barrier = pltpu.get_barrier_semaphore()

    def greet(device):
        pl.semaphore_signal(barrier, inc=1, device_id={"bus": device}, device_id_type=MESH)

    has_prev(lambda: greet(me - 1))
    has_next(lambda: greet(me + 1))
    for j in range(1, outer_n):
        greet(((outer + j) % outer_n) * INNER + inner)
    greet(sib)
    greet(pair)
    own_copy = pltpu.make_async_copy(schur, s_win.at[1], own_sem)
    own_copy.start()
    edges = jnp.where(me > 0, 1, 0) + jnp.where(me < n - 1, 1, 0)
    pl.semaphore_wait(barrier, outer_n + 1 + edges)

    to_prev, to_next = [], []
    step = if_rows // (CHUNKS // 2)
    for k in range(CHUNKS):
        at = (k * 2 // CHUNKS, pl.ds(k % (CHUNKS // 2) * step, step))
        src = schur.at[at]
        to_prev.append(
            remote(src, s_win.at[(2,) + at], s_send.at[0, k], s_recv.at[0, k], me - 1)
        )
        to_next.append(
            remote(src, s_win.at[(0,) + at], s_send.at[1, k], s_recv.at[1, k], me + 1)
        )

    def start_chunks(first, last):
        for k in range(first, last):
            has_prev(to_prev[k].start)
            has_next(to_next[k].start)

    start_chunks(0, 8)

    for fetch in fetches:
        fetch.wait()
    slot = slots[...]
    kind = types[...]
    hit = lax.broadcasted_iota(jnp.int32, (bus_rows, bus_rows), 0) == slot
    ones = jnp.where(hit, 1.0, 0.0)
    perm[...] = ones.T.astype(BF16)
    place = ones.astype(BF16)
    load_place = jnp.where(kind == 0, ones, 0.0).astype(BF16)
    first_place = jnp.where(kind <= 1, ones, 0.0).astype(BF16)
    placed = one_sided(load_place, loads[...])
    first = one_sided(first_place, loads[...])
    low = low_half((bus_rows, columns))
    drv[...] = jnp.where(low, first, -first)
    other = swap(placed)
    mul_same[...] = jnp.where(low, -placed, other)
    mul_swap[...] = jnp.where(low, other, placed)

    branches = branch_bus.shape[1]
    at_bus = lax.broadcasted_iota(jnp.int32, (bus_rows, branches), 0) == branch_bus[...]
    spread = dot(place, jnp.where(at_bus, 1.0, 0.0).astype(BF16)).astype(BF16)
    relative = branch_iface[...] - (me - 1) * if_rows
    at_row = lax.broadcasted_iota(jnp.int32, (pad, branches), 0) == relative
    weights = jnp.concatenate(
        [jnp.where(at_row, adm[0:1, :], 0.0), jnp.where(at_row, adm[1:2, :], 0.0)], axis=0
    )
    weights_high, weights_low = split(weights)
    joins = dot_nt(weights_high, spread) + dot_nt(weights_low, spread)
    for p in range(parts):
        cols = slice(p * pb, (p + 1) * pb)
        inv_re, inv_im = block_inverse[p, 0], block_inverse[p, 1]
        high, lowp = split(jnp.concatenate([inv_re, inv_im], axis=0))
        b_high[p] = high
        b_low[p] = lowp
        g = joins[:, cols]
        q = dot3(g, jnp.concatenate([inv_re, inv_im], axis=1), dot)
        w_re = q[:rows3, :pb] - q[pad : pad + rows3, pb:]
        w_im = q[:rows3, pb:] + q[pad : pad + rows3, :pb]
        high, lowp = split(jnp.concatenate([w_re, w_im], axis=0))
        w_high[:, cols] = high
        w_low[:, cols] = lowp

    joined[...] = joins

    window_ref[rows3:, :] = jnp.zeros((pad - rows3, columns), F32)

    @pl.when(me == 0)
    def _():
        window_ref[:if_rows, :] = jnp.zeros((if_rows, columns), F32)
        s_win[0] = jnp.zeros(s_win.shape[1:], F32)
        nb[:, 0] = jnp.zeros((ORDERS, if_rows, columns), F32)

    @pl.when(me == n - 1)
    def _():
        window_ref[2 * if_rows : rows3, :] = jnp.zeros((if_rows, columns), F32)
        s_win[2] = jnp.zeros(s_win.shape[1:], F32)
        nb[:, 1] = jnp.zeros((ORDERS, if_rows, columns), F32)

    def order(t, carry):
        x = drv[...]
        near[t] = complex_apply(w_high[...], w_low[...], x)
        lower = remote(
            near.at[t, pl.ds(0, if_rows)], nb.at[t, 1], nb_send.at[t, 0], nb_recv.at[t, 0], me - 1
        )
        upper = remote(
            near.at[t, pl.ds(2 * if_rows, if_rows)],
            nb.at[t, 0], nb_send.at[t, 1], nb_recv.at[t, 1], me + 1,
        )
        has_prev(lower.start)
        has_next(upper.start)
        for p in range(parts):
            at = slice(p * pb, (p + 1) * pb)
            coeffs[t, at, :] = complex_apply(b_high[p], b_low[p], x[at])
        has_next(lower.wait_recv)
        has_prev(upper.wait_recv)
        gath[t, me] = near[t, if_rows : 2 * if_rows, :] + (nb[t, 0] + nb[t, 1])

        sends = []
        z_copies = []
        for j in range(1, outer_n):
            to = ((outer + j) % outer_n) * INNER + inner
            block = gath.at[t, me]
            copy = remote(block, block, z_send.at[t, j], z_recv.at[t, j], to)
            copy.start()
            z_copies.append(copy)
        pl.when(t == 0)(lambda: start_chunks(8, 12))
        y_copies = []
        for j in range(outer_n):
            if j:
                z_copies[j - 1].wait_recv()
            came = ((outer - j + outer_n) % outer_n) * INNER + inner
            block = gath.at[t, came]
            copy = remote(block, block, y_send.at[t, j], y_recv.at[t, j], pair)
            copy.start()
            y_copies.append(copy)
            copy = remote(block, block, c_send.at[t, j], c_recv.at[t, j], sib)
            copy.start()
            sends.append(copy)

        def earlier(k, total):
            return total + complex_mul(coeffs[k], terms[t - 1 - k])

        past = lax.fori_loop(0, t, earlier, jnp.zeros((bus_rows, columns), F32))
        terms[t] = -past

        @pl.when(t == 0)
        def _():
            own_copy.wait()
            for part in range(2):
                at = part * if_rows
                high, lowp = split(s_win[1, part])
                own_high[at : at + if_rows, :] = high
                own_low[at : at + if_rows, :] = lowp
            for p in range(parts):
                inv_re, inv_im = block_inverse[p, 0], block_inverse[p, 1]
                g = joined[:, p * pb : (p + 1) * pb]
                r = dot3(jnp.concatenate([inv_re, inv_im], axis=0), g, dot_nt)
                high, lowp = split(r[:pb, :pad] - r[pb:, pad:])
                h_high[p * pb : (p + 1) * pb, :] = high
                h_low[p * pb : (p + 1) * pb, :] = lowp
                high, lowp = split(r[:pb, pad:] + r[pb:, :pad])
                at = bus_rows + p * pb
                h_high[at : at + pb, :] = high
                h_low[at : at + pb, :] = lowp

        @pl.when(t == 1)
        def _():
            for k in range(CHUNKS):
                has_next(to_prev[k].wait_recv)
                has_prev(to_next[k].wait_recv)
            for part in range(2):
                for w in range(3):
                    at = (part * 3 + w) * if_rows
                    high, lowp = split(s_win[w, part])
                    s_high[at : at + if_rows, :] = high
                    s_low[at : at + if_rows, :] = lowp

        f_copies = []
        for j in range(outer_n):
            y_copies[j].wait_recv()
            came = ((outer - j + outer_n) % outer_n) * INNER + pair_inner
            block = gath.at[t, came]
            copy = remote(block, block, f_send.at[t, j], f_recv.at[t, j], sib)
            copy.start()
            f_copies.append(copy)
        pl.when(t == 0)(lambda: start_chunks(12, CHUNKS))
        for copy in sends + f_copies:
            copy.wait_recv()

        sums = gath[t].reshape(n * if_rows, columns)

        @pl.when(t == 0)
        def _():
            own_if[...] = complex_apply(own_high[...], own_low[...], sums)
            down = remote(
                own_if, window_ref.at[pl.ds(2 * if_rows, if_rows)],
                i_send.at[0], i_recv.at[0], me - 1,
            )
            up = remote(own_if, window_ref.at[pl.ds(0, if_rows)], i_send.at[1], i_recv.at[1], me + 1)
            has_prev(down.start)
            has_next(up.start)
            window_ref[if_rows : 2 * if_rows, :] = own_if[...]
            has_next(down.wait_recv)
            has_prev(up.wait_recv)
            has_prev(down.wait_send)
            has_next(up.wait_send)

        @pl.when(t > 0)
        def _():
            window_ref[:rows3, :] = complex_apply(s_high[...], s_low[...], sums)

        coeff = coeffs[t] + complex_apply(h_high[...], h_low[...], window_ref[...])
        coeffs[t] = coeff
        term = coeff + terms[t]
        terms[t] = term
        drv[...] = mul_same[...] * term + mul_swap[...] * swap(term)

        has_prev(lower.wait_send)
        has_next(upper.wait_send)
        for copy in z_copies + y_copies + sends + f_copies:
            copy.wait_send()
        return carry

    lax.fori_loop(0, ORDERS, order, 0)

    for k in range(CHUNKS):
        has_prev(to_prev[k].wait_send)
        has_next(to_next[k].wait_send)
    total = jnp.where(low, 1.0, 0.0)
    for k in range(ORDERS):
        total = total + coeffs[k]
    voltage_out[...] = one_sided(perm[...], total)
    last_out[...] = one_sided(perm[...], coeffs[ORDERS - 1])


def local(
    loads, bus_type, bus_slot, block_inverse, schur_inverse, branch_bus, branch_iface, branch_adm
):
    n = lax.axis_size("bus")
    bus_rows, columns = loads.shape
    if_rows, iface = schur_inverse.shape[1:]
    parts, _, pb, _ = block_inverse.shape
    branches = branch_bus.shape[0]
    rows3 = 3 * if_rows
    outer_n = n // INNER
    pad = -(-rows3 // 128) * 128
    vmem = pl.BlockSpec(memory_space=pltpu.VMEM)
    dma = pltpu.SemaphoreType.DMA
    out = jax.ShapeDtypeStruct((bus_rows, columns), F32)
    return pl.pallas_call(
        functools.partial(kernel, n),
        out_shape=(out, out),
        in_specs=[pl.BlockSpec(memory_space=pl.ANY)] * 8,
        out_specs=(vmem, vmem),
        scratch_shapes=[
            pltpu.VMEM((bus_rows, columns), F32),
            pltpu.VMEM((1, bus_rows), jnp.int32),
            pltpu.VMEM((1, bus_rows), jnp.int32),
            pltpu.VMEM(block_inverse.shape, F32),
            pltpu.VMEM((1, branches), jnp.int32),
            pltpu.VMEM((1, branches), jnp.int32),
            pltpu.VMEM((2, branches), F32),
            dma((7,)),
            pltpu.VMEM((2 * pad, bus_rows), F32),
            pltpu.VMEM((2 * if_rows, iface), BF16),
            pltpu.VMEM((2 * if_rows, iface), BF16),
            pltpu.VMEM((if_rows, columns), F32),
            pltpu.VMEM((pad, columns), F32),
            dma((2,)), dma((2,)),
            pltpu.VMEM((bus_rows, bus_rows), BF16),
            pltpu.VMEM((bus_rows, columns), F32),
            pltpu.VMEM((bus_rows, columns), F32),
            pltpu.VMEM((bus_rows, columns), F32),
            pltpu.VMEM((2 * rows3, bus_rows), BF16),
            pltpu.VMEM((2 * rows3, bus_rows), BF16),
            pltpu.VMEM((2 * bus_rows, pad), BF16),
            pltpu.VMEM((2 * bus_rows, pad), BF16),
            pltpu.VMEM((parts, 2 * pb, pb), BF16),
            pltpu.VMEM((parts, 2 * pb, pb), BF16),
            pltpu.VMEM((3, 2, if_rows, iface), F32),
            pltpu.VMEM((2 * rows3, iface), BF16),
            pltpu.VMEM((2 * rows3, iface), BF16),
            pltpu.VMEM((ORDERS, bus_rows, columns), F32),
            pltpu.VMEM((ORDERS, bus_rows, columns), F32),
            pltpu.VMEM((ORDERS, rows3, columns), F32),
            pltpu.VMEM((ORDERS, 2, if_rows, columns), F32),
            pltpu.VMEM((ORDERS, n, if_rows, columns), F32),
            dma, dma((2, CHUNKS)), dma((2, CHUNKS)),
            dma((ORDERS, 2)), dma((ORDERS, 2)),
            dma((ORDERS, outer_n)), dma((ORDERS, outer_n)),
            dma((ORDERS, outer_n)), dma((ORDERS, outer_n)),
            dma((ORDERS, outer_n)), dma((ORDERS, outer_n)),
            dma((ORDERS, outer_n)), dma((ORDERS, outer_n)),
        ],
        compiler_params=pltpu.CompilerParams(
            collective_id=0, has_side_effects=True, vmem_limit_bytes=56 * 1024 * 1024
        ),
        name="power_flow",
    )(
        loads,
        bus_type.reshape(1, bus_rows),
        bus_slot.reshape(1, bus_rows),
        block_inverse,
        schur_inverse,
        branch_bus.reshape(1, -1),
        branch_iface.reshape(1, -1),
        branch_adm,
    )


def solution(mesh):
    in_specs = (
        P(("grp", "bus"), None),
        P(("grp", "bus")),
        P(("grp", "bus")),
        P(("grp", "bus"), None, None, None),
        P(None, ("grp", "bus"), None),
        P(("grp", "bus")),
        P(("grp", "bus")),
        P(None, ("grp", "bus")),
    )
    out_specs = (P(("grp", "bus"), None), P(("grp", "bus"), None))
    return jax.shard_map(local, mesh=mesh, in_specs=in_specs, out_specs=out_specs, check_vma=False)
```

```python
import functools

import jax
import jax.numpy as jnp
from jax import lax
from jax.experimental import pallas as pl
from jax.experimental.pallas import tpu as pltpu
from jax.sharding import PartitionSpec as P

ORDERS = 4
INNER = 4
CHUNKS = 16
F32 = jnp.float32
BF16 = jnp.bfloat16
MESH = pl.DeviceIdType.MESH


def dot(a, b):
    return lax.dot_general(a, b, (((1,), (0,)), ((), ())), preferred_element_type=F32)


def dot_nt(a, b):
    return lax.dot_general(a, b, (((1,), (1,)), ((), ())), preferred_element_type=F32)


def split(x):
    high = x.astype(BF16)
    return high, (x - high.astype(F32)).astype(BF16)


def low_half(shape):
    return lax.broadcasted_iota(jnp.int32, shape, 1) < shape[1] // 2


def swap(x):
    return pltpu.roll(x, x.shape[1] // 2, 1)


def rotate(x):
    other = swap(x)
    return jnp.where(low_half(x.shape), -other, other)


def one_sided(select, x):
    high, low = split(x)
    out = dot(select, jnp.concatenate([high, low], axis=1))
    width = x.shape[1]
    return out[:, :width] + out[:, width:]


def dot3(a, b, mul):
    a_high, a_low = split(a)
    b_high, b_low = split(b)
    return mul(a_high, b_high) + (mul(a_high, b_low) + mul(a_low, b_high))


def complex_apply(high, low, x):
    width = x.shape[1]
    x_high, x_low = split(x)
    both = dot(high, jnp.concatenate([x_high, x_low], axis=1))
    out = both[:, :width] + (both[:, width:] + dot(low, x_high))
    rows = out.shape[0] // 2
    return out[:rows] + rotate(out[rows:])


def complex_mul(a, b):
    other = swap(a)
    low = low_half(a.shape)
    real = jnp.where(low, a, other)
    imag = jnp.where(low, -other, a)
    return real * b + imag * swap(b)


def kernel(
    n,
    loads_in, types_in, slots_in, inverse_in, schur, bus_in, iface_in, adm_in,
    voltage_out, last_out,
    loads, types, slots, block_inverse, branch_bus, branch_iface, adm, in_sem,
    joined, own_high, own_low, own_if, window_ref, i_send, i_recv,
    perm, drv, mul_same, mul_swap, w_high, w_low, h_high, h_low, b_high, b_low,
    s_win, s_high, s_low, coeffs, terms, near, nb, gath,
    own_sem, s_send, s_recv, nb_send, nb_recv, z_send, z_recv, y_send, y_recv,
    c_send, c_recv, f_send, f_recv,
):
    outer_n = n // INNER
    me = lax.axis_index("bus")
    outer = me // INNER
    inner = me % INNER
    sib = me + 1 - 2 * (me % 2)
    pair = me + 2 - 4 * ((me // 2) % 2)
    pair_inner = pair % INNER
    bus_rows, columns = loads.shape
    if_rows = schur.shape[1]
    parts, pb = block_inverse.shape[0], block_inverse.shape[2]
    rows3 = 3 * if_rows
    pad = h_high.shape[1]

    def remote(src, dst, send, recv, device):
        return pltpu.make_async_remote_copy(
            src_ref=src, dst_ref=dst, send_sem=send, recv_sem=recv,
            device_id={"bus": device}, device_id_type=MESH,
        )

    def has_prev(fn):
        pl.when(me > 0)(fn)

    def has_next(fn):
        pl.when(me < n - 1)(fn)

    arrays = (
        (slots_in, slots), (types_in, types), (loads_in, loads), (bus_in, branch_bus),
        (iface_in, branch_iface), (adm_in, adm), (inverse_in, block_inverse),
    )
    fetches = [
        pltpu.make_async_copy(src, dst, in_sem.at[i]) for i, (src, dst) in enumerate(arrays)
    ]
    for fetch in fetches:
        fetch.start()
    barrier = pltpu.get_barrier_semaphore()

    def greet(device):
        pl.semaphore_signal(barrier, inc=1, device_id={"bus": device}, device_id_type=MESH)

    has_prev(lambda: greet(me - 1))
    has_next(lambda: greet(me + 1))
    for j in range(1, outer_n):
        greet(((outer + j) % outer_n) * INNER + inner)
    greet(sib)
    greet(pair)
    own_copy = pltpu.make_async_copy(schur, s_win.at[1], own_sem)
    own_copy.start()
    edges = jnp.where(me > 0, 1, 0) + jnp.where(me < n - 1, 1, 0)
    pl.semaphore_wait(barrier, outer_n + 1 + edges)

    to_prev, to_next = [], []
    step = if_rows // (CHUNKS // 2)
    for k in range(CHUNKS):
        at = (k * 2 // CHUNKS, pl.ds(k % (CHUNKS // 2) * step, step))
        src = schur.at[at]
        to_prev.append(
            remote(src, s_win.at[(2,) + at], s_send.at[0, k], s_recv.at[0, k], me - 1)
        )
        to_next.append(
            remote(src, s_win.at[(0,) + at], s_send.at[1, k], s_recv.at[1, k], me + 1)
        )

    def start_chunks(first, last):
        for k in range(first, last):
            has_prev(to_prev[k].start)
            has_next(to_next[k].start)

    start_chunks(0, 8)

    for fetch in fetches:
        fetch.wait()
    slot = slots[...]
    kind = types[...]
    hit = lax.broadcasted_iota(jnp.int32, (bus_rows, bus_rows), 0) == slot
    ones = jnp.where(hit, 1.0, 0.0)
    place = ones.astype(BF16)
    load_place = jnp.where(kind == 0, ones, 0.0).astype(BF16)
    first_place = jnp.where(kind <= 1, ones, 0.0).astype(BF16)
    placed = one_sided(load_place, loads[...])
    first = one_sided(first_place, loads[...])
    low = low_half((bus_rows, columns))
    drv[...] = jnp.where(low, first, -first)
    other = swap(placed)
    mul_same[...] = jnp.where(low, -placed, other)
    mul_swap[...] = jnp.where(low, other, placed)

    branches = branch_bus.shape[1]
    at_bus = lax.broadcasted_iota(jnp.int32, (bus_rows, branches), 0) == branch_bus[...]
    spread = dot(place, jnp.where(at_bus, 1.0, 0.0).astype(BF16)).astype(BF16)
    relative = branch_iface[...] - (me - 1) * if_rows
    at_row = lax.broadcasted_iota(jnp.int32, (pad, branches), 0) == relative
    weights = jnp.concatenate(
        [jnp.where(at_row, adm[0:1, :], 0.0), jnp.where(at_row, adm[1:2, :], 0.0)], axis=0
    )
    weights_high, weights_low = split(weights)
    joins = dot_nt(weights_high, spread) + dot_nt(weights_low, spread)
    for p in range(parts):
        cols = slice(p * pb, (p + 1) * pb)
        inv_re, inv_im = block_inverse[p, 0], block_inverse[p, 1]
        g = joins[:, cols]
        q = dot3(g, jnp.concatenate([inv_re, inv_im], axis=1), dot)
        w_re = q[:rows3, :pb] - q[pad : pad + rows3, pb:]
        w_im = q[:rows3, pb:] + q[pad : pad + rows3, :pb]
        mid = slice(if_rows, 2 * if_rows)
        ends = (slice(0, if_rows), slice(2 * if_rows, rows3))
        w = [w_re[at] for at in ends] + [w_im[at] for at in ends] + [w_re[mid], w_im[mid]]
        high, lowp = split(jnp.concatenate(w, axis=0))
        w_high[:, cols] = high
        w_low[:, cols] = lowp

    joined[...] = joins

    window_ref[rows3:, :] = jnp.zeros((pad - rows3, columns), F32)

    @pl.when(me == 0)
    def _():
        window_ref[:if_rows, :] = jnp.zeros((if_rows, columns), F32)
        s_win[0] = jnp.zeros(s_win.shape[1:], F32)
        nb[:, 0] = jnp.zeros((ORDERS, if_rows, columns), F32)

    @pl.when(me == n - 1)
    def _():
        window_ref[2 * if_rows : rows3, :] = jnp.zeros((if_rows, columns), F32)
        s_win[2] = jnp.zeros(s_win.shape[1:], F32)
        nb[:, 1] = jnp.zeros((ORDERS, if_rows, columns), F32)

    def order(t, carry):
        x = drv[...]
        cut = 4 * if_rows
        near[t, : 2 * if_rows, :] = complex_apply(w_high[:cut, :], w_low[:cut, :], x)
        lower = remote(
            near.at[t, pl.ds(0, if_rows)], nb.at[t, 1], nb_send.at[t, 0], nb_recv.at[t, 0], me - 1
        )
        upper = remote(
            near.at[t, pl.ds(if_rows, if_rows)],
            nb.at[t, 0], nb_send.at[t, 1], nb_recv.at[t, 1], me + 1,
        )
        has_prev(lower.start)
        has_next(upper.start)
        near[t, 2 * if_rows :, :] = complex_apply(w_high[cut:, :], w_low[cut:, :], x)

        @pl.when(t == 0)
        def _():
            for p in range(parts):
                stacked = block_inverse[p].reshape(2 * pb, pb)
                b_high[p], b_low[p] = split(stacked)

        for p in range(parts):
            at = slice(p * pb, (p + 1) * pb)
            coeffs[t, at, :] = complex_apply(b_high[p], b_low[p], x[at])
        has_next(lower.wait_recv)
        has_prev(upper.wait_recv)
        gath[t, me] = near[t, 2 * if_rows :, :] + (nb[t, 0] + nb[t, 1])

        sends = []
        z_copies = []
        steps = sorted(range(1, outer_n), key=lambda j: (min(j, outer_n - j), j))
        for j in steps:
            to = ((outer + j) % outer_n) * INNER + inner
            block = gath.at[t, me]
            copy = remote(block, block, z_send.at[t, j], z_recv.at[t, j], to)
            copy.start()
            z_copies.append(copy)
        pl.when(t == 0)(lambda: start_chunks(8, 12))
        y_copies = []
        for i, j in enumerate([0] + steps):
            if i:
                z_copies[i - 1].wait_recv()
            came = ((outer - j + outer_n) % outer_n) * INNER + inner
            block = gath.at[t, came]
            copy = remote(block, block, y_send.at[t, j], y_recv.at[t, j], pair)
            copy.start()
            y_copies.append(copy)
            copy = remote(block, block, c_send.at[t, j], c_recv.at[t, j], sib)
            copy.start()
            sends.append(copy)

        def earlier(k, total):
            return total + complex_mul(coeffs[k], terms[t - 1 - k])

        past = lax.fori_loop(0, t, earlier, jnp.zeros((bus_rows, columns), F32))
        terms[t] = -past

        @pl.when(t == 0)
        def _():
            own_copy.wait()
            rows = lax.broadcasted_iota(jnp.int32, (bus_rows, bus_rows), 0)
            perm[...] = jnp.where(rows == slots[...], 1.0, 0.0).T.astype(BF16)
            for part in range(2):
                at = part * if_rows
                high, lowp = split(s_win[1, part])
                own_high[at : at + if_rows, :] = high
                own_low[at : at + if_rows, :] = lowp
            for p in range(parts):
                inv_re, inv_im = block_inverse[p, 0], block_inverse[p, 1]
                g = joined[:, p * pb : (p + 1) * pb]
                r = dot3(jnp.concatenate([inv_re, inv_im], axis=0), g, dot_nt)
                high, lowp = split(r[:pb, :pad] - r[pb:, pad:])
                h_high[p * pb : (p + 1) * pb, :] = high
                h_low[p * pb : (p + 1) * pb, :] = lowp
                high, lowp = split(r[:pb, pad:] + r[pb:, :pad])
                at = bus_rows + p * pb
                h_high[at : at + pb, :] = high
                h_low[at : at + pb, :] = lowp

        @pl.when(t == 1)
        def _():
            for k in range(CHUNKS):
                has_next(to_prev[k].wait_recv)
                has_prev(to_next[k].wait_recv)
            for part in range(2):
                for w in range(3):
                    at = (part * 3 + w) * if_rows
                    high, lowp = split(s_win[w, part])
                    s_high[at : at + if_rows, :] = high
                    s_low[at : at + if_rows, :] = lowp

        f_copies = []
        for i, j in enumerate([0] + steps):
            y_copies[i].wait_recv()
            came = ((outer - j + outer_n) % outer_n) * INNER + pair_inner
            block = gath.at[t, came]
            copy = remote(block, block, f_send.at[t, j], f_recv.at[t, j], sib)
            copy.start()
            f_copies.append(copy)
        pl.when(t == 0)(lambda: start_chunks(12, CHUNKS))
        group = INNER * if_rows

        def arrived(i):
            j = ([0] + steps)[i]
            sends[i].wait_recv()
            f_copies[i].wait_recv()
            came = (outer - j + outer_n) % outer_n
            cols = pl.ds(pl.multiple_of(came * group, group), group)
            return cols, gath[t, pl.ds(came * INNER, INNER)].reshape(group, columns)


        @pl.when(t == 0)
        def _():
            total = None
            for j in range(outer_n):
                cols, sums = arrived(j)
                part = complex_apply(own_high[:, cols], own_low[:, cols], sums)
                total = part if total is None else total + part
            own_if[...] = total
            down = remote(
                own_if, window_ref.at[pl.ds(2 * if_rows, if_rows)],
                i_send.at[0], i_recv.at[0], me - 1,
            )
            up = remote(own_if, window_ref.at[pl.ds(0, if_rows)], i_send.at[1], i_recv.at[1], me + 1)
            has_prev(down.start)
            has_next(up.start)
            window_ref[if_rows : 2 * if_rows, :] = own_if[...]
            has_next(down.wait_recv)
            has_prev(up.wait_recv)
            has_prev(down.wait_send)
            has_next(up.wait_send)

        @pl.when(t > 0)
        def _():
            total = None
            for j in range(outer_n):
                cols, sums = arrived(j)
                part = complex_apply(s_high[:, cols], s_low[:, cols], sums)
                total = part if total is None else total + part
            window_ref[:rows3, :] = total

        coeff = coeffs[t] + complex_apply(h_high[...], h_low[...], window_ref[...])
        coeffs[t] = coeff
        term = coeff + terms[t]
        terms[t] = term
        drv[...] = mul_same[...] * term + mul_swap[...] * swap(term)

        has_prev(lower.wait_send)
        has_next(upper.wait_send)
        for copy in z_copies + y_copies + sends + f_copies:
            copy.wait_send()
        return carry

    lax.fori_loop(0, ORDERS, order, 0)

    for k in range(CHUNKS):
        has_prev(to_prev[k].wait_send)
        has_next(to_next[k].wait_send)
    total = jnp.where(low, 1.0, 0.0)
    for k in range(ORDERS):
        total = total + coeffs[k]
    voltage_out[...] = one_sided(perm[...], total)
    last_out[...] = one_sided(perm[...], coeffs[ORDERS - 1])


def local(
    loads, bus_type, bus_slot, block_inverse, schur_inverse, branch_bus, branch_iface, branch_adm
):
    n = lax.axis_size("bus")
    bus_rows, columns = loads.shape
    if_rows, iface = schur_inverse.shape[1:]
    parts, _, pb, _ = block_inverse.shape
    branches = branch_bus.shape[0]
    rows3 = 3 * if_rows
    outer_n = n // INNER
    pad = -(-rows3 // 128) * 128
    vmem = pl.BlockSpec(memory_space=pltpu.VMEM)
    dma = pltpu.SemaphoreType.DMA
    out = jax.ShapeDtypeStruct((bus_rows, columns), F32)
    return pl.pallas_call(
        functools.partial(kernel, n),
        out_shape=(out, out),
        in_specs=[pl.BlockSpec(memory_space=pl.ANY)] * 8,
        out_specs=(vmem, vmem),
        scratch_shapes=[
            pltpu.VMEM((bus_rows, columns), F32),
            pltpu.VMEM((1, bus_rows), jnp.int32),
            pltpu.VMEM((1, bus_rows), jnp.int32),
            pltpu.VMEM(block_inverse.shape, F32),
            pltpu.VMEM((1, branches), jnp.int32),
            pltpu.VMEM((1, branches), jnp.int32),
            pltpu.VMEM((2, branches), F32),
            dma((7,)),
            pltpu.VMEM((2 * pad, bus_rows), F32),
            pltpu.VMEM((2 * if_rows, iface), BF16),
            pltpu.VMEM((2 * if_rows, iface), BF16),
            pltpu.VMEM((if_rows, columns), F32),
            pltpu.VMEM((pad, columns), F32),
            dma((2,)), dma((2,)),
            pltpu.VMEM((bus_rows, bus_rows), BF16),
            pltpu.VMEM((bus_rows, columns), F32),
            pltpu.VMEM((bus_rows, columns), F32),
            pltpu.VMEM((bus_rows, columns), F32),
            pltpu.VMEM((2 * rows3, bus_rows), BF16),
            pltpu.VMEM((2 * rows3, bus_rows), BF16),
            pltpu.VMEM((2 * bus_rows, pad), BF16),
            pltpu.VMEM((2 * bus_rows, pad), BF16),
            pltpu.VMEM((parts, 2 * pb, pb), BF16),
            pltpu.VMEM((parts, 2 * pb, pb), BF16),
            pltpu.VMEM((3, 2, if_rows, iface), F32),
            pltpu.VMEM((2 * rows3, iface), BF16),
            pltpu.VMEM((2 * rows3, iface), BF16),
            pltpu.VMEM((ORDERS, bus_rows, columns), F32),
            pltpu.VMEM((ORDERS, bus_rows, columns), F32),
            pltpu.VMEM((ORDERS, rows3, columns), F32),
            pltpu.VMEM((ORDERS, 2, if_rows, columns), F32),
            pltpu.VMEM((ORDERS, n, if_rows, columns), F32),
            dma, dma((2, CHUNKS)), dma((2, CHUNKS)),
            dma((ORDERS, 2)), dma((ORDERS, 2)),
            dma((ORDERS, outer_n)), dma((ORDERS, outer_n)),
            dma((ORDERS, outer_n)), dma((ORDERS, outer_n)),
            dma((ORDERS, outer_n)), dma((ORDERS, outer_n)),
            dma((ORDERS, outer_n)), dma((ORDERS, outer_n)),
        ],
        compiler_params=pltpu.CompilerParams(
            collective_id=0, has_side_effects=True, vmem_limit_bytes=56 * 1024 * 1024
        ),
        name="power_flow",
    )(
        loads,
        bus_type.reshape(1, bus_rows),
        bus_slot.reshape(1, bus_rows),
        block_inverse,
        schur_inverse,
        branch_bus.reshape(1, -1),
        branch_iface.reshape(1, -1),
        branch_adm,
    )


def solution(mesh):
    in_specs = (
        P(("grp", "bus"), None),
        P(("grp", "bus")),
        P(("grp", "bus")),
        P(("grp", "bus"), None, None, None),
        P(None, ("grp", "bus"), None),
        P(("grp", "bus")),
        P(("grp", "bus")),
        P(None, ("grp", "bus")),
    )
    out_specs = (P(("grp", "bus"), None), P(("grp", "bus"), None))
    return jax.shard_map(local, mesh=mesh, in_specs=in_specs, out_specs=out_specs, check_vma=False)
```

```python
import functools

import jax
import jax.numpy as jnp
from jax import lax
from jax.experimental import pallas as pl
from jax.experimental.pallas import tpu as pltpu
from jax.sharding import PartitionSpec as P

ORDERS = 4
INNER = 4
CHUNKS = 16
F32 = jnp.float32
BF16 = jnp.bfloat16
MESH = pl.DeviceIdType.MESH


def dot(a, b):
    return lax.dot_general(a, b, (((1,), (0,)), ((), ())), preferred_element_type=F32)


def dot_nt(a, b):
    return lax.dot_general(a, b, (((1,), (1,)), ((), ())), preferred_element_type=F32)


def split(x):
    high = x.astype(BF16)
    return high, (x - high.astype(F32)).astype(BF16)


def low_half(shape):
    return lax.broadcasted_iota(jnp.int32, shape, 1) < shape[1] // 2


def swap(x):
    return pltpu.roll(x, x.shape[1] // 2, 1)


def rotate(x):
    other = swap(x)
    return jnp.where(low_half(x.shape), -other, other)


def one_sided(select, x):
    high, low = split(x)
    out = dot(select, jnp.concatenate([high, low], axis=1))
    width = x.shape[1]
    return out[:, :width] + out[:, width:]


def dot3(a, b, mul):
    a_high, a_low = split(a)
    b_high, b_low = split(b)
    return mul(a_high, b_high) + (mul(a_high, b_low) + mul(a_low, b_high))


def complex_apply(high, low, x):
    width = x.shape[1]
    x_high, x_low = split(x)
    both = dot(high, jnp.concatenate([x_high, x_low], axis=1))
    out = both[:, :width] + (both[:, width:] + dot(low, x_high))
    rows = out.shape[0] // 2
    return out[:rows] + rotate(out[rows:])


def complex_mul(a, b):
    other = swap(a)
    low = low_half(a.shape)
    real = jnp.where(low, a, other)
    imag = jnp.where(low, -other, a)
    return real * b + imag * swap(b)


def kernel(
    n,
    loads_in, types_in, slots_in, inverse_in, schur, bus_in, iface_in, adm_in,
    voltage_out, last_out,
    loads, types, slots, block_inverse, branch_bus, branch_iface, adm, in_sem,
    joined, own_high, own_low, own_if, window_ref, i_send, i_recv,
    perm, drv, mul_same, mul_swap, w_high, w_low, h_high, h_low, b_high, b_low,
    s_win, s_high, s_low, coeffs, terms, near, nb, gath,
    own_sem, s_send, s_recv, nb_send, nb_recv, z_send, z_recv, y_send, y_recv,
    c_send, c_recv, f_send, f_recv,
):
    outer_n = n // INNER
    me = lax.axis_index("bus")
    outer = me // INNER
    inner = me % INNER
    sib = me + 1 - 2 * (me % 2)
    pair = me + 2 - 4 * ((me // 2) % 2)
    pair_inner = pair % INNER
    bus_rows, columns = loads.shape
    if_rows = schur.shape[1]
    parts, pb = block_inverse.shape[0], block_inverse.shape[2]
    rows3 = 3 * if_rows
    pad = h_high.shape[1]

    def remote(src, dst, send, recv, device):
        return pltpu.make_async_remote_copy(
            src_ref=src, dst_ref=dst, send_sem=send, recv_sem=recv,
            device_id={"bus": device}, device_id_type=MESH,
        )

    def has_prev(fn):
        pl.when(me > 0)(fn)

    def has_next(fn):
        pl.when(me < n - 1)(fn)

    arrays = (
        (slots_in, slots), (types_in, types), (loads_in, loads), (bus_in, branch_bus),
        (iface_in, branch_iface), (adm_in, adm), (inverse_in, block_inverse),
    )
    fetches = [
        pltpu.make_async_copy(src, dst, in_sem.at[i]) for i, (src, dst) in enumerate(arrays)
    ]
    for fetch in fetches:
        fetch.start()
    barrier = pltpu.get_barrier_semaphore()

    def greet(device):
        pl.semaphore_signal(barrier, inc=1, device_id={"bus": device}, device_id_type=MESH)

    has_prev(lambda: greet(me - 1))
    has_next(lambda: greet(me + 1))
    for j in range(1, outer_n):
        greet(((outer + j) % outer_n) * INNER + inner)
    greet(sib)
    greet(pair)
    own_copy = pltpu.make_async_copy(schur, s_win.at[1], own_sem)
    own_copy.start()
    edges = jnp.where(me > 0, 1, 0) + jnp.where(me < n - 1, 1, 0)
    pl.semaphore_wait(barrier, outer_n + 1 + edges)

    to_prev, to_next = [], []
    step = if_rows // (CHUNKS // 2)
    for k in range(CHUNKS):
        at = (k * 2 // CHUNKS, pl.ds(k % (CHUNKS // 2) * step, step))
        src = schur.at[at]
        to_prev.append(
            remote(src, s_win.at[(2,) + at], s_send.at[0, k], s_recv.at[0, k], me - 1)
        )
        to_next.append(
            remote(src, s_win.at[(0,) + at], s_send.at[1, k], s_recv.at[1, k], me + 1)
        )

    def start_chunks(first, last):
        for k in range(first, last):
            has_prev(to_prev[k].start)
            has_next(to_next[k].start)

    start_chunks(0, 8)

    for fetch in fetches:
        fetch.wait()
    slot = slots[...]
    kind = types[...]
    hit = lax.broadcasted_iota(jnp.int32, (bus_rows, bus_rows), 0) == slot
    ones = jnp.where(hit, 1.0, 0.0)
    place = ones.astype(BF16)
    load_place = jnp.where(kind == 0, ones, 0.0).astype(BF16)
    first_place = jnp.where(kind <= 1, ones, 0.0).astype(BF16)
    placed = one_sided(load_place, loads[...])
    first = one_sided(first_place, loads[...])
    low = low_half((bus_rows, columns))
    drv[...] = jnp.where(low, first, -first)
    other = swap(placed)
    mul_same[...] = jnp.where(low, -placed, other)
    mul_swap[...] = jnp.where(low, other, placed)

    branches = branch_bus.shape[1]
    at_bus = lax.broadcasted_iota(jnp.int32, (bus_rows, branches), 0) == branch_bus[...]
    spread = dot(place, jnp.where(at_bus, 1.0, 0.0).astype(BF16)).astype(BF16)
    relative = branch_iface[...] - (me - 1) * if_rows
    at_row = lax.broadcasted_iota(jnp.int32, (pad, branches), 0) == relative
    weights = jnp.concatenate(
        [jnp.where(at_row, adm[0:1, :], 0.0), jnp.where(at_row, adm[1:2, :], 0.0)], axis=0
    )
    weights_high, weights_low = split(weights)
    joins = dot_nt(weights_high, spread) + dot_nt(weights_low, spread)
    for p in range(parts):
        cols = slice(p * pb, (p + 1) * pb)
        inv_re, inv_im = block_inverse[p, 0], block_inverse[p, 1]
        g = joins[:, cols]
        q = dot3(g, jnp.concatenate([inv_re, inv_im], axis=1), dot)
        w_re = q[:rows3, :pb] - q[pad : pad + rows3, pb:]
        w_im = q[:rows3, pb:] + q[pad : pad + rows3, :pb]
        mid = slice(if_rows, 2 * if_rows)
        ends = (slice(0, if_rows), slice(2 * if_rows, rows3))
        w = [w_re[at] for at in ends] + [w_im[at] for at in ends] + [w_re[mid], w_im[mid]]
        high, lowp = split(jnp.concatenate(w, axis=0))
        w_high[:, cols] = high
        w_low[:, cols] = lowp

    joined[...] = joins

    window_ref[rows3:, :] = jnp.zeros((pad - rows3, columns), F32)

    @pl.when(me == 0)
    def _():
        window_ref[:if_rows, :] = jnp.zeros((if_rows, columns), F32)
        s_win[0] = jnp.zeros(s_win.shape[1:], F32)
        nb[:, 0] = jnp.zeros((ORDERS, if_rows, columns), F32)

    @pl.when(me == n - 1)
    def _():
        window_ref[2 * if_rows : rows3, :] = jnp.zeros((if_rows, columns), F32)
        s_win[2] = jnp.zeros(s_win.shape[1:], F32)
        nb[:, 1] = jnp.zeros((ORDERS, if_rows, columns), F32)

    def order(t, carry):
        x = drv[...]
        cut = 4 * if_rows
        near[t, : 2 * if_rows, :] = complex_apply(w_high[:cut, :], w_low[:cut, :], x)
        lower = remote(
            near.at[t, pl.ds(0, if_rows)], nb.at[t, 1], nb_send.at[t, 0], nb_recv.at[t, 0], me - 1
        )
        upper = remote(
            near.at[t, pl.ds(if_rows, if_rows)],
            nb.at[t, 0], nb_send.at[t, 1], nb_recv.at[t, 1], me + 1,
        )
        has_prev(lower.start)
        has_next(upper.start)
        near[t, 2 * if_rows :, :] = complex_apply(w_high[cut:, :], w_low[cut:, :], x)

        @pl.when(t == 0)
        def _():
            for p in range(parts):
                stacked = block_inverse[p].reshape(2 * pb, pb)
                b_high[p], b_low[p] = split(stacked)

        for p in range(parts):
            at = slice(p * pb, (p + 1) * pb)
            coeffs[t, at, :] = complex_apply(b_high[p], b_low[p], x[at])
        has_next(lower.wait_recv)
        has_prev(upper.wait_recv)
        gath[t, me] = near[t, 2 * if_rows :, :] + (nb[t, 0] + nb[t, 1])

        sends = []
        z_copies = []
        steps = sorted(range(1, outer_n), key=lambda j: (min(j, outer_n - j), j))
        for j in steps:
            to = ((outer + j) % outer_n) * INNER + inner
            block = gath.at[t, me]
            copy = remote(block, block, z_send.at[t, j], z_recv.at[t, j], to)
            copy.start()
            z_copies.append(copy)
        pl.when(t == 0)(lambda: start_chunks(8, 12))
        y_copies = []
        for i, j in enumerate([0] + steps):
            if i:
                z_copies[i - 1].wait_recv()
            came = ((outer - j + outer_n) % outer_n) * INNER + inner
            block = gath.at[t, came]
            copy = remote(block, block, y_send.at[t, j], y_recv.at[t, j], pair)
            copy.start()
            y_copies.append(copy)
            copy = remote(block, block, c_send.at[t, j], c_recv.at[t, j], sib)
            copy.start()
            sends.append(copy)

        def earlier(k, total):
            return total + complex_mul(coeffs[k], terms[t - 1 - k])

        past = lax.fori_loop(0, t, earlier, jnp.zeros((bus_rows, columns), F32))
        terms[t] = -past

        @pl.when(t == 0)
        def _():
            own_copy.wait()
            rows = lax.broadcasted_iota(jnp.int32, (bus_rows, bus_rows), 0)
            perm[...] = jnp.where(rows == slots[...], 1.0, 0.0).T.astype(BF16)
            for part in range(2):
                at = part * if_rows
                high, lowp = split(s_win[1, part])
                own_high[at : at + if_rows, :] = high
                own_low[at : at + if_rows, :] = lowp
            for p in range(parts):
                inv_re, inv_im = block_inverse[p, 0], block_inverse[p, 1]
                g = joined[:, p * pb : (p + 1) * pb]
                r = dot3(jnp.concatenate([inv_re, inv_im], axis=0), g, dot_nt)
                high, lowp = split(r[:pb, :pad] - r[pb:, pad:])
                h_high[p * pb : (p + 1) * pb, :] = high
                h_low[p * pb : (p + 1) * pb, :] = lowp
                high, lowp = split(r[:pb, pad:] + r[pb:, :pad])
                at = bus_rows + p * pb
                h_high[at : at + pb, :] = high
                h_low[at : at + pb, :] = lowp

        @pl.when(t == ORDERS - 1)
        def _():
            total = jnp.where(low_half((bus_rows, columns)), 1.0, 0.0)
            for k in range(ORDERS - 1):
                total = total + coeffs[k]
            voltage_out[...] = one_sided(perm[...], total)

        @pl.when(t == 1)
        def _():
            for k in range(CHUNKS):
                has_next(to_prev[k].wait_recv)
                has_prev(to_next[k].wait_recv)
            for part in range(2):
                for w in range(3):
                    at = (part * 3 + w) * if_rows
                    high, lowp = split(s_win[w, part])
                    s_high[at : at + if_rows, :] = high
                    s_low[at : at + if_rows, :] = lowp

        f_copies = []
        for i, j in enumerate([0] + steps):
            y_copies[i].wait_recv()
            came = ((outer - j + outer_n) % outer_n) * INNER + pair_inner
            block = gath.at[t, came]
            copy = remote(block, block, f_send.at[t, j], f_recv.at[t, j], sib)
            copy.start()
            f_copies.append(copy)
        pl.when(t == 0)(lambda: start_chunks(12, CHUNKS))
        group = INNER * if_rows

        def arrived(i):
            j = ([0] + steps)[i]
            sends[i].wait_recv()
            f_copies[i].wait_recv()
            came = (outer - j + outer_n) % outer_n
            cols = pl.ds(pl.multiple_of(came * group, group), group)
            return cols, gath[t, pl.ds(came * INNER, INNER)].reshape(group, columns)


        @pl.when(t == 0)
        def _():
            total = None
            for j in range(outer_n):
                cols, sums = arrived(j)
                part = complex_apply(own_high[:, cols], own_low[:, cols], sums)
                total = part if total is None else total + part
            own_if[...] = total
            down = remote(
                own_if, window_ref.at[pl.ds(2 * if_rows, if_rows)],
                i_send.at[0], i_recv.at[0], me - 1,
            )
            up = remote(own_if, window_ref.at[pl.ds(0, if_rows)], i_send.at[1], i_recv.at[1], me + 1)
            has_prev(down.start)
            has_next(up.start)
            window_ref[if_rows : 2 * if_rows, :] = own_if[...]
            has_next(down.wait_recv)
            has_prev(up.wait_recv)
            has_prev(down.wait_send)
            has_next(up.wait_send)

        @pl.when(t > 0)
        def _():
            total = None
            for j in range(outer_n):
                cols, sums = arrived(j)
                part = complex_apply(s_high[:, cols], s_low[:, cols], sums)
                total = part if total is None else total + part
            window_ref[:rows3, :] = total

        coeff = coeffs[t] + complex_apply(h_high[...], h_low[...], window_ref[...])
        coeffs[t] = coeff

        @pl.when(t < ORDERS - 1)
        def _():
            term = coeffs[t] + terms[t]
            terms[t] = term
            drv[...] = mul_same[...] * term + mul_swap[...] * swap(term)

        has_prev(lower.wait_send)
        has_next(upper.wait_send)
        for copy in z_copies + y_copies + sends + f_copies:
            copy.wait_send()
        return carry

    lax.fori_loop(0, ORDERS, order, 0)

    for k in range(CHUNKS):
        has_prev(to_prev[k].wait_send)
        has_next(to_next[k].wait_send)
    last = one_sided(perm[...], coeffs[ORDERS - 1])
    last_out[...] = last
    voltage_out[...] += last


def local(
    loads, bus_type, bus_slot, block_inverse, schur_inverse, branch_bus, branch_iface, branch_adm
):
    n = lax.axis_size("bus")
    bus_rows, columns = loads.shape
    if_rows, iface = schur_inverse.shape[1:]
    parts, _, pb, _ = block_inverse.shape
    branches = branch_bus.shape[0]
    rows3 = 3 * if_rows
    outer_n = n // INNER
    pad = -(-rows3 // 128) * 128
    vmem = pl.BlockSpec(memory_space=pltpu.VMEM)
    dma = pltpu.SemaphoreType.DMA
    out = jax.ShapeDtypeStruct((bus_rows, columns), F32)
    return pl.pallas_call(
        functools.partial(kernel, n),
        out_shape=(out, out),
        in_specs=[pl.BlockSpec(memory_space=pl.ANY)] * 8,
        out_specs=(vmem, vmem),
        scratch_shapes=[
            pltpu.VMEM((bus_rows, columns), F32),
            pltpu.VMEM((1, bus_rows), jnp.int32),
            pltpu.VMEM((1, bus_rows), jnp.int32),
            pltpu.VMEM(block_inverse.shape, F32),
            pltpu.VMEM((1, branches), jnp.int32),
            pltpu.VMEM((1, branches), jnp.int32),
            pltpu.VMEM((2, branches), F32),
            dma((7,)),
            pltpu.VMEM((2 * pad, bus_rows), F32),
            pltpu.VMEM((2 * if_rows, iface), BF16),
            pltpu.VMEM((2 * if_rows, iface), BF16),
            pltpu.VMEM((if_rows, columns), F32),
            pltpu.VMEM((pad, columns), F32),
            dma((2,)), dma((2,)),
            pltpu.VMEM((bus_rows, bus_rows), BF16),
            pltpu.VMEM((bus_rows, columns), F32),
            pltpu.VMEM((bus_rows, columns), F32),
            pltpu.VMEM((bus_rows, columns), F32),
            pltpu.VMEM((2 * rows3, bus_rows), BF16),
            pltpu.VMEM((2 * rows3, bus_rows), BF16),
            pltpu.VMEM((2 * bus_rows, pad), BF16),
            pltpu.VMEM((2 * bus_rows, pad), BF16),
            pltpu.VMEM((parts, 2 * pb, pb), BF16),
            pltpu.VMEM((parts, 2 * pb, pb), BF16),
            pltpu.VMEM((3, 2, if_rows, iface), F32),
            pltpu.VMEM((2 * rows3, iface), BF16),
            pltpu.VMEM((2 * rows3, iface), BF16),
            pltpu.VMEM((ORDERS, bus_rows, columns), F32),
            pltpu.VMEM((ORDERS, bus_rows, columns), F32),
            pltpu.VMEM((ORDERS, rows3, columns), F32),
            pltpu.VMEM((ORDERS, 2, if_rows, columns), F32),
            pltpu.VMEM((ORDERS, n, if_rows, columns), F32),
            dma, dma((2, CHUNKS)), dma((2, CHUNKS)),
            dma((ORDERS, 2)), dma((ORDERS, 2)),
            dma((ORDERS, outer_n)), dma((ORDERS, outer_n)),
            dma((ORDERS, outer_n)), dma((ORDERS, outer_n)),
            dma((ORDERS, outer_n)), dma((ORDERS, outer_n)),
            dma((ORDERS, outer_n)), dma((ORDERS, outer_n)),
        ],
        compiler_params=pltpu.CompilerParams(
            collective_id=0, has_side_effects=True, vmem_limit_bytes=56 * 1024 * 1024
        ),
        name="power_flow",
    )(
        loads,
        bus_type.reshape(1, bus_rows),
        bus_slot.reshape(1, bus_rows),
        block_inverse,
        schur_inverse,
        branch_bus.reshape(1, -1),
        branch_iface.reshape(1, -1),
        branch_adm,
    )


def solution(mesh):
    in_specs = (
        P(("grp", "bus"), None),
        P(("grp", "bus")),
        P(("grp", "bus")),
        P(("grp", "bus"), None, None, None),
        P(None, ("grp", "bus"), None),
        P(("grp", "bus")),
        P(("grp", "bus")),
        P(None, ("grp", "bus")),
    )
    out_specs = (P(("grp", "bus"), None), P(("grp", "bus"), None))
    return jax.shard_map(local, mesh=mesh, in_specs=in_specs, out_specs=out_specs, check_vma=False)
```
